256 devices in a mesh: stripe: 16 (over y, x_hi, core), dev: 16 (over z, x_lo).
Axes of the slice: x: 4 (x_hi: 2, x_lo: 2; x = x_hi * 2 + x_lo), y: 4, z: 8, core: 2. Of those that a mesh axis runs over, the one named last changes fastest.
Arguments:
- row_factors: float32 [16384, 128], P(('stripe', 'dev')), may hold values from -1.8 to 1.8
- col_factors: float32 [262144, 128], P(('stripe', 'dev')), may hold values from -1.8 to 1.8
- ratings: bfloat16 [3, 8192, 128, 128], P(None, ('stripe', 'dev')), may hold values from -6 to 6
- rating_mask: int32 [3, 8192, 128, 128], P(None, ('stripe', 'dev')), may hold values 0 or 1
- tile_rows: int32 [3, 8192], P(None, ('stripe', 'dev')), may hold values from 0 to 7
- tile_cols: int32 [3, 8192], P(None, ('stripe', 'dev')), may hold values from 0 to 7
- tile_count: int32 [3, 256], P(None, ('stripe', 'dev')), may hold values from 1 to 32, as said below
Outputs:
- row_out: float32 [16384, 128], P(('stripe', 'dev'))
- col_out: float32 [262144, 128], P(('stripe', 'dev'))
The draws below stay inside these ranges and needn't reach their ends.
Inputs may be any that keep to these rules, and one draw needn't show every extreme that they name: `tile_count`: slots past a device's count are padding. In every stratum some device has all 32 slots live.
All inputs are finite; a program needn't handle non-finite values. No bound on the sum of `rating_mask` on one device may be relied on, other than what follows from the above.
Results may differ from the reference program's by a relative error of at most 0.0003.
Values may be sent and summed in bfloat16 or wider, within the bound.
A program may use at most 128 MiB of HBM per device.

```python
import jax
import jax.numpy as jnp
from jax import lax

K = 128
TILE = 128
RT = 8
CT = 8
NT = 32
STRATA = 3
ROWS = 16384
COLS = 262144
TILES = 8192
N_STRIPE = 16
N_DEV = 16
DEVICES = 256


def draw_tile_count(key, part):
    first_key, second_key, third_key = jax.random.split(key, 3)
    first_draw = jax.random.randint(first_key, (STRATA, DEVICES), 1, NT + 1)
    second_draw = jax.random.randint(second_key, (STRATA, DEVICES), 1, NT + 1)
    counts = jnp.minimum(first_draw, second_draw)
    busiest = jax.random.randint(third_key, (STRATA, 1), 0, DEVICES)
    counts = jnp.where(jnp.arange(DEVICES, dtype=jnp.int32)[None, :] == busiest, NT, counts)
    return counts.astype(jnp.int32)


def place_ends(entries, stream_key, smallest, top_value):
    longest = entries.shape.index(max(entries.shape))
    spots = []
    for shift in (0, 1):
        where = [jax.random.randint(jax.random.fold_in(stream_key, axis), (), 0, length) for axis, length in enumerate(entries.shape)]
        where[longest] = (where[longest] + shift) % entries.shape[longest]
        spots.append(tuple(where))
    return entries.at[spots[0]].set(smallest).at[spots[1]].set(top_value)


def block_levels(rng, shape, pieces, smallest, top_value):
    def one(dim, shards_of):
        draws = jax.random.uniform(jax.random.fold_in(jax.random.fold_in(rng, 6), dim), (shards_of,), jnp.float32, smallest / len(pieces), top_value / len(pieces))
        return jnp.repeat(jnp.exp(draws), shape[dim] // shards_of).reshape((-1,) + (1,) * (len(shape) - dim - 1))

    level = one(*pieces[0])
    for cut in pieces[1:]:
        level = level * one(*cut)
    return level


def centred(stream_key, extent, deviation, most, cuts=(), held_as=jnp.bfloat16):
    array = deviation * jax.random.normal(stream_key, extent, jnp.float32)
    if cuts:
        array = array * block_levels(stream_key, extent, cuts, -0.22, 0.18)
    return jnp.clip(array, -most, most).astype(held_as)


def setup_inputs(seed: int = 0) -> dict:
    arg_keys = jax.random.split(jax.random.key(seed), 8)
    row_factors = centred(arg_keys[0], (ROWS, K), 0.3, 1.8, ((0, 256),), jnp.float32)
    col_factors = centred(arg_keys[1], (COLS, K), 0.3, 1.8, ((0, 256),), jnp.float32)
    ratings = centred(arg_keys[2], (STRATA, TILES, TILE, TILE), 1.0, 6.0, ((1, 256),))
    rating_mask = place_ends((jax.random.randint(arg_keys[3], (STRATA, TILES, TILE, TILE), 0, 2) < 1).astype(jnp.int32), jax.random.fold_in(arg_keys[3], 1), 0, 1)
    tile_rows = place_ends(jax.random.randint(arg_keys[4], (STRATA, TILES), 0, RT), jax.random.fold_in(arg_keys[4], 1), 0, RT - 1).astype(jnp.int32)
    tile_cols = place_ends(jax.random.randint(arg_keys[5], (STRATA, TILES), 0, CT), jax.random.fold_in(arg_keys[5], 1), 0, CT - 1).astype(jnp.int32)
    tile_count = draw_tile_count(jax.random.fold_in(arg_keys[7], 71), 0)
    return {"row_factors": row_factors, "col_factors": col_factors, "ratings": ratings, "rating_mask": rating_mask, "tile_rows": tile_rows, "tile_cols": tile_cols, "tile_count": tile_count}


learn_rate = 0.02
ridge_weight = 2.5


def reference(row_factors, col_factors, ratings, rating_mask, tile_rows, tile_cols, tile_count):
    devices = N_STRIPE * N_DEV
    shrink = 1.0 - learn_rate * ridge_weight
    stripes = row_factors.reshape(N_STRIPE, RT, TILE, K)
    held_blocks = col_factors.reshape(devices, CT, TILE, K)
    device_ids = jnp.arange(devices, dtype=jnp.int32)
    stripe_of = device_ids // N_DEV
    slot_ids = jnp.arange(NT, dtype=jnp.int32)
    for stratum in range(STRATA):
        row_index = tile_rows[stratum].reshape(devices, NT)
        col_index = tile_cols[stratum].reshape(devices, NT)
        left_tiles = stripes[stripe_of[:, None], row_index]
        right_tiles = held_blocks[device_ids[:, None], col_index]
        live_flags = slot_ids[None, :] < tile_count[stratum][:, None]
        rating_tiles = ratings[stratum].reshape(devices, NT, TILE, TILE).astype(jnp.float32)
        observed = rating_mask[stratum].reshape(devices, NT, TILE, TILE) > 0
        keep_entry = jnp.logical_and(observed, live_flags[:, :, None, None])
        predicted = jnp.einsum("dnik,dnjk->dnij", left_tiles, right_tiles, precision=lax.Precision.HIGHEST)
        residual = jnp.where(keep_entry, predicted - rating_tiles, jnp.float32(0.0))
        row_grad = jnp.einsum("dnij,dnjk->dnik", residual, right_tiles, precision=lax.Precision.HIGHEST)
        col_grad = jnp.einsum("dnij,dnik->dnjk", residual, left_tiles, precision=lax.Precision.HIGHEST)
        grad_stripes = jnp.zeros((N_STRIPE, RT, TILE, K), jnp.float32).at[stripe_of[:, None], row_index].add(row_grad)
        grad_blocks = jnp.zeros((devices, CT, TILE, K), jnp.float32).at[device_ids[:, None], col_index].add(col_grad)
        stripes = shrink * stripes - learn_rate * grad_stripes
        held_blocks = shrink * held_blocks - learn_rate * grad_blocks
        moved = jnp.roll(held_blocks.reshape(N_STRIPE, N_DEV, CT, TILE, K), 1, axis=0)
        held_blocks = moved.reshape(devices, CT, TILE, K)
    return stripes.reshape(ROWS, K), held_blocks.reshape(COLS, K)
```

```python
import functools

import jax
import jax.numpy as jnp
from jax import lax
from jax.experimental import pallas as pl
from jax.experimental.pallas import tpu as pltpu
from jax.sharding import PartitionSpec as P

MESH = pl.DeviceIdType.MESH
STRATA = 3
LEARN_RATE = 0.02
RIDGE_WEIGHT = 2.5
SHRINK = 1.0 - LEARN_RATE * RIDGE_WEIGHT
F32, BF16, I16 = jnp.float32, jnp.bfloat16, jnp.int16
TOP = 32767.0
NT = (((1,), (1,)), ((), ()))
NN = (((1,), (0,)), ((), ()))
TN = (((0,), (0,)), ((), ()))


def mm(a, b, dims):
    return lax.dot_general(a, b, dims, preferred_element_type=F32)


def split(x):
    hi = x.astype(BF16)
    return hi, (x - hi.astype(F32)).astype(BF16)


def quantize(x):
    peak = jnp.maximum(jnp.max(jnp.abs(x), axis=0, keepdims=True), 1e-30)
    code = jnp.round(x * (TOP / peak)).astype(jnp.int32).astype(I16)
    return code, peak * (1.0 / TOP)


def decode(code, scale):
    return code.astype(jnp.int32).astype(F32) * scale


def kernel(
    n_stripe, n_dev, order_s, start_s, own_ref, h0_ref, rat_ref, mask_ref, uout_ref, hout_ref,
    rat_a, rat_b, rat_c, mask_a, mask_b, mask_c, psm, psr, u2, hhh, hcat, e_hi, e_lo, hbuf, own, g_tile, g_own,
    rs_src, rs_src_sc, rs_dst, rs_dst_sc, ag_src, ag_src_sc, ag_dst, ag_dst_sc,
    in_sem, rs_ss, rs_rs, rs_ss2, rs_rs2, ag_ss, ag_rs, ag_ss2, ag_rs2, h_ss, h_rs,
):
    s, d = lax.axis_index("stripe"), lax.axis_index("dev")
    z, lo = d // 2, d % 2
    ahead = (s + 1) % n_stripe
    behind = (s + n_stripe - 1) % n_stripe

    barrier = pltpu.get_barrier_semaphore()
    for k in range(1, n_dev):
        pl.semaphore_signal(barrier, inc=1, device_id=(s, (d + k) % n_dev), device_id_type=MESH)
    for other in (ahead, behind):
        pl.semaphore_signal(barrier, inc=1, device_id=(other, d), device_id_type=MESH)

    rat_v, mask_v = (rat_a, rat_b, rat_c), (mask_a, mask_b, mask_c)
    loads = []
    for t in range(STRATA):
        loads.append((
            pltpu.make_async_copy(rat_ref.at[t], rat_v[t], in_sem.at[2 * t]),
            pltpu.make_async_copy(mask_ref.at[t], mask_v[t], in_sem.at[2 * t + 1]),
        ))
        for load in loads[t]:
            load.start()

    def set_u(rows, x):
        hi, low = split(x)
        u2[rows, 0:128] = hi
        u2[rows, 128:256] = low

    def set_h(source):
        def body(c, carry):
            rows = pl.ds(pl.multiple_of(c * 128, 128), 128)
            hi, low = split(source[rows, :])
            hhh[rows, 0:128] = hi
            hhh[rows, 128:256] = hi
            hcat[rows, 0:128] = hi
            hcat[rows, 128:256] = low
            return carry

        lax.fori_loop(0, 8, body, 0)

    def prefix(t):
        for load in loads[t]:
            load.wait()

        def body(i, carry):
            slot = order_s[t, i]
            seen = mask_v[t][slot] > 0
            value = jnp.where(seen, rat_v[t][slot].astype(F32), 0.0)
            psm[i + 1] = psm[i] + jnp.where(seen, 1.0, 0.0)
            psr[i + 1] = psr[i] + value
            return carry

        lax.fori_loop(0, 32, body, 0)

    def rs_copy(j):
        return (
            pltpu.make_async_remote_copy(
                src_ref=rs_src.at[j], dst_ref=rs_dst.at[d], send_sem=rs_ss.at[j], recv_sem=rs_rs.at[d],
                device_id=(s, j), device_id_type=MESH),
            pltpu.make_async_remote_copy(
                src_ref=rs_src_sc.at[j], dst_ref=rs_dst_sc.at[d], send_sem=rs_ss2.at[j], recv_sem=rs_rs2.at[d],
                device_id=(s, j), device_id_type=MESH),
        )

    def rs_arrival(j):
        return (
            pltpu.make_async_remote_copy(
                src_ref=rs_src.at[j], dst_ref=rs_dst.at[j], send_sem=rs_ss.at[j], recv_sem=rs_rs.at[j],
                device_id=(s, j), device_id_type=MESH),
            pltpu.make_async_remote_copy(
                src_ref=rs_src_sc.at[j], dst_ref=rs_dst_sc.at[j], send_sem=rs_ss2.at[j], recv_sem=rs_rs2.at[j],
                device_id=(s, j), device_id_type=MESH),
        )

    def ag_copy(j):
        return (
            pltpu.make_async_remote_copy(
                src_ref=ag_src, dst_ref=ag_dst.at[d], send_sem=ag_ss.at[j], recv_sem=ag_rs.at[d],
                device_id=(s, j), device_id_type=MESH),
            pltpu.make_async_remote_copy(
                src_ref=ag_src_sc, dst_ref=ag_dst_sc.at[d], send_sem=ag_ss2.at[j], recv_sem=ag_rs2.at[d],
                device_id=(s, j), device_id_type=MESH),
        )

    def ag_arrival(j):
        return (
            pltpu.make_async_remote_copy(
                src_ref=ag_src, dst_ref=ag_dst.at[j], send_sem=ag_ss.at[j], recv_sem=ag_rs.at[j],
                device_id=(s, j), device_id_type=MESH),
            pltpu.make_async_remote_copy(
                src_ref=ag_src_sc, dst_ref=ag_dst_sc.at[j], send_sem=ag_ss2.at[j], recv_sem=ag_rs2.at[j],
                device_id=(s, j), device_id_type=MESH),
        )

    def far_first(i):
        return 4 + (i // 2) - (i % 2) * (2 * (i // 2) + 1)

    def ag_send():
        for k in (8, 9, 7, 6, 10, 5, 11, 4, 12, 3, 13, 2, 14, 1, 15):
            j = (d + k) % n_dev
            for copy in ag_copy(j):
                copy.start()

    def ag_prepare():
        rows = pl.ds(pl.multiple_of(d * 64, 64), 64)
        code, scale = quantize(own[...])
        ag_src[...] = code
        ag_src_sc[...] = scale
        set_u(rows, own[...])

    def ag_take():
        def body(k, carry):
            j = (d + k) % n_dev
            for copy in ag_arrival(j):
                copy.wait_recv()
            set_u(pl.ds(pl.multiple_of(j * 64, 64), 64), decode(ag_dst[j], ag_dst_sc[j]))
            return carry

        lax.fori_loop(1, n_dev, body, 0)

        def drain(k, carry):
            for copy in ag_copy((d + k) % n_dev):
                copy.wait_send()
            return carry

        lax.fori_loop(1, n_dev, drain, 0)

    def row_tile(t, r):
        rows = pl.ds(pl.multiple_of(r * 128, 128), 128)
        u_both = u2[rows, :]
        u_hi = u2[rows, 0:128]
        for c in range(4):
            cols = slice(c * 256, (c + 1) * 256)
            pred = mm(u_both, hhh[cols, :], NT) + mm(u_hi, hcat[cols, 128:256], NT)
            for half in range(2):
                cell = r * 8 + c * 2 + half
                begin, end = start_s[t, cell], start_s[t, cell + 1]
                weight = psm[end] - psm[begin]
                total = psr[end] - psr[begin]
                err = weight * pred[:, half * 128:(half + 1) * 128] - total
                hi, low = split(err)
                at = slice(c * 256 + half * 128, c * 256 + half * 128 + 128)
                e_hi[rows, at] = hi
                e_lo[rows, at] = low
        both = mm(e_hi[rows, :], hcat[...], NN)
        return both[:, 0:128] + both[:, 128:256] + mm(e_lo[rows, :], hcat[:, 0:128], NN)

    def phase1(t):
        def body(i, carry):
            r = (z + far_first(i)) % 8
            g_tile[...] = row_tile(t, r)
            for half in range(2):
                j = 2 * r + half
                code, scale = quantize(g_tile[half * 64:(half + 1) * 64, :])
                rs_src[j] = code
                rs_src_sc[j] = scale
                for copy in rs_copy(j):
                    copy.start()
            return carry

        lax.fori_loop(0, 7, body, 0)
        g_tile[...] = row_tile(t, z)
        other = d + 1 - 2 * lo
        code, scale = quantize(g_tile[pl.ds(pl.multiple_of((1 - lo) * 64, 64), 64), :])
        rs_src[other] = code
        rs_src_sc[other] = scale
        for copy in rs_copy(other):
            copy.start()
        g_own[...] = g_tile[pl.ds(pl.multiple_of(lo * 64, 64), 64), :]

    def h_copy(t, c):
        rows = pl.ds(pl.multiple_of(c * 128, 128), 128)
        target = hbuf.at[t + 1, rows] if t + 1 < STRATA else hout_ref.at[rows]
        return pltpu.make_async_remote_copy(
            src_ref=hbuf.at[t, rows], dst_ref=target, send_sem=h_ss.at[8 * t + c], recv_sem=h_rs.at[8 * t + c],
            device_id=(ahead, d), device_id_type=MESH)

    def phase2(t):
        def body(c, carry):
            cols = pl.ds(pl.multiple_of(c * 128, 128), 128)
            both = mm(e_hi[:, cols], u2[...], TN)
            grad = both[:, 0:128] + both[:, 128:256] + mm(e_lo[:, cols], u2[:, 0:128], TN)
            old = h0_ref[cols, :] if t == 0 else hbuf[t, cols, :]
            hbuf[t, cols, :] = SHRINK * old - LEARN_RATE * grad
            h_copy(t, c).start()
            return carry

        lax.fori_loop(0, 8, body, 0)

    def rs_sum():
        def body(k, total):
            j = (d + k) % n_dev
            for copy in rs_arrival(j):
                copy.wait_recv()
            return total + decode(rs_dst[j], rs_dst_sc[j])

        total = lax.fori_loop(1, n_dev, body, g_own[...])
        own[...] = SHRINK * own[...] - LEARN_RATE * total

        def drain(k, carry):
            for copy in rs_copy((d + k) % n_dev):
                copy.wait_send()
            return carry

        lax.fori_loop(1, n_dev, drain, 0)

    own[...] = own_ref[...]
    psm[0] = jnp.zeros_like(psm[0])
    psr[0] = jnp.zeros_like(psr[0])
    ag_prepare()
    pl.semaphore_wait(barrier, n_dev + 1)
    ag_send()
    set_h(h0_ref)
    prefix(0)
    ag_take()
    for t in range(STRATA):
        phase1(t)
        phase2(t)
        if t + 1 < STRATA:
            prefix(t + 1)
        rs_sum()
        if t + 1 < STRATA:
            ag_prepare()
            ag_send()

            def landed(c, carry):
                h_copy(t, c).wait_recv()
                return carry

            lax.fori_loop(0, 8, landed, 0)
            set_h(hbuf.at[t + 1])
            ag_take()
    uout_ref[...] = own[...]

    def landed(c, carry):
        h_copy(STRATA - 1, c).wait_recv()
        return carry

    lax.fori_loop(0, 8, landed, 0)
    for t in range(STRATA):

        def sent(c, carry):
            h_copy(t, c).wait_send()
            return carry

        lax.fori_loop(0, 8, sent, 0)


def tile_lists(tile_rows, tile_cols, tile_count):
    slots = tile_rows.shape[1]
    index = jnp.arange(slots, dtype=jnp.int32)
    key = jnp.where(index[None, :] < tile_count, tile_rows * 8 + tile_cols, 64)
    unique = key * slots + index[None, :]
    rank = jnp.sum((unique[:, None, :] < unique[:, :, None]).astype(jnp.int32), axis=2)
    order = jnp.sum(jnp.where(rank[:, None, :] == index[None, :, None], index[None, None, :], 0), axis=2)
    cells = jnp.arange(72, dtype=jnp.int32)
    start = jnp.sum((key[:, None, :] < cells[None, :, None]).astype(jnp.int32), axis=2)
    return order, start


def shards(n_stripe, n_dev, row_factors, col_factors, ratings, rating_mask, tile_rows, tile_cols, tile_count):
    order, start = tile_lists(tile_rows, tile_cols, tile_count)
    vmem, smem, anywhere = (pl.BlockSpec(memory_space=m) for m in (pltpu.VMEM, pltpu.SMEM, pl.ANY))
    dma = lambda n: pltpu.SemaphoreType.DMA((n,))
    return pl.pallas_call(
        functools.partial(kernel, n_stripe, n_dev),
        out_shape=(
            jax.ShapeDtypeStruct(row_factors.shape, F32),
            jax.ShapeDtypeStruct(col_factors.shape, F32),
        ),
        in_specs=[smem, smem, vmem, vmem, anywhere, anywhere],
        out_specs=(vmem, anywhere),
        scratch_shapes=[
            *[pltpu.VMEM((32, 128, 128), BF16)] * 3,
            *[pltpu.VMEM((32, 128, 128), jnp.int32)] * 3,
            pltpu.VMEM((33, 128, 128), F32),
            pltpu.VMEM((33, 128, 128), F32),
            pltpu.VMEM((1024, 256), BF16),
            pltpu.VMEM((1024, 256), BF16),
            pltpu.VMEM((1024, 256), BF16),
            pltpu.VMEM((1024, 1024), BF16),
            pltpu.VMEM((1024, 1024), BF16),
            pltpu.VMEM((3, 1024, 128), F32),
            pltpu.VMEM((64, 128), F32),
            pltpu.VMEM((128, 128), F32),
            pltpu.VMEM((64, 128), F32),
            pltpu.VMEM((16, 64, 128), I16),
            pltpu.VMEM((16, 1, 128), F32),
            pltpu.VMEM((16, 64, 128), I16),
            pltpu.VMEM((16, 1, 128), F32),
            pltpu.VMEM((64, 128), I16),
            pltpu.VMEM((1, 128), F32),
            pltpu.VMEM((16, 64, 128), I16),
            pltpu.VMEM((16, 1, 128), F32),
            dma(6), dma(16), dma(16), dma(16), dma(16), dma(16), dma(16), dma(16), dma(16), dma(24), dma(24),
        ],
        compiler_params=pltpu.CompilerParams(
            collective_id=0, has_side_effects=True, vmem_limit_bytes=56 * 1024 * 1024
        ),
    )(order, start, row_factors, col_factors, ratings, rating_mask)


def solution(mesh):
    in_specs = (
        P(("stripe", "dev"), None),
        P(("stripe", "dev"), None),
        P(None, ("stripe", "dev"), None, None),
        P(None, ("stripe", "dev"), None, None),
        P(None, ("stripe", "dev")),
        P(None, ("stripe", "dev")),
        P(None, ("stripe", "dev")),
    )
    out_specs = (P(("stripe", "dev"), None), P(("stripe", "dev"), None))
    body = functools.partial(shards, mesh.shape["stripe"], mesh.shape["dev"])
    return jax.shard_map(body, mesh=mesh, in_specs=in_specs, out_specs=out_specs, check_vma=False)
```

```python
import functools

import jax
import jax.numpy as jnp
from jax import lax
from jax.experimental import pallas as pl
from jax.experimental.pallas import tpu as pltpu
from jax.sharding import PartitionSpec as P

MESH = pl.DeviceIdType.MESH
STRATA = 3
LEARN_RATE = 0.02
RIDGE_WEIGHT = 2.5
SHRINK = 1.0 - LEARN_RATE * RIDGE_WEIGHT
F32, BF16, I16 = jnp.float32, jnp.bfloat16, jnp.int16
TOP = 32767.0
NT = (((1,), (1,)), ((), ()))
NN = (((1,), (0,)), ((), ()))
TN = (((0,), (0,)), ((), ()))


def mm(a, b, dims):
    return lax.dot_general(a, b, dims, preferred_element_type=F32)


def split(x):
    hi = x.astype(BF16)
    return hi, (x - hi.astype(F32)).astype(BF16)


def quantize(x):
    peak = jnp.maximum(jnp.max(jnp.abs(x), axis=0, keepdims=True), 1e-30)
    code = jnp.round(x * (TOP / peak)).astype(jnp.int32).astype(I16)
    return code, peak * (1.0 / TOP)


def decode(code, scale):
    return code.astype(jnp.int32).astype(F32) * scale


def kernel(
    n_stripe, n_dev, order_s, start_s, own_ref, h0_ref, rat_ref, mask_ref, uout_ref, code_ref, scale_ref,
    rat_v, mask_v, psm, psr, dm, dr, u3, h3, hcat, e_hi, e_lo, hcur, own, g_tile, g_own,
    rs_src, rs_src_sc, rs_dst, rs_dst_sc, ag_src, ag_src_sc, ag_dst, ag_dst_sc, h_src, h_src_sc, h_dst, h_dst_sc,
    in_sem, rs_ss, rs_rs, rs_ss2, rs_rs2, ag_ss, ag_rs, ag_ss2, ag_rs2, h_ss, h_rs, h_ss2, h_rs2,
):
    s, d = lax.axis_index("stripe"), lax.axis_index("dev")
    ahead = lax.rem(s + 1, n_stripe)
    behind = lax.rem(s + n_stripe - 1, n_stripe)
    far_first = (8, 9, 7, 6, 10, 5, 11, 4, 12, 3, 13, 2, 14, 1, 15)

    def peer(k):
        return lax.rem(d + k, n_dev)

    barrier = pltpu.get_barrier_semaphore()
    for k in range(1, n_dev):
        pl.semaphore_signal(barrier, inc=1, device_id=(s, peer(k)), device_id_type=MESH)
    for other in (ahead, behind):
        pl.semaphore_signal(barrier, inc=1, device_id=(other, d), device_id_type=MESH)

    def loads(t):
        return (
            pltpu.make_async_copy(rat_ref.at[t], rat_v, in_sem.at[0]),
            pltpu.make_async_copy(mask_ref.at[t], mask_v, in_sem.at[1]),
        )

    def load(t):
        for copy in loads(t):
            copy.start()

    def set_h(value, save):
        def body(c, carry):
            rows = pl.ds(pl.multiple_of(c * 128, 128), 128)
            x = value(c, rows)
            if save:
                hcur[rows, :] = x
            hi, low = split(x)
            hcat[rows, 0:128] = hi
            hcat[rows, 128:256] = low
            hi, low = split(x.T)
            h3[0:128, rows] = hi
            h3[128:256, rows] = hi
            h3[256:384, rows] = low
            return carry

        lax.fori_loop(0, 8, body, 0)

    def prefix(t):
        for copy in loads(t):
            copy.wait()

        def body(i, carry):
            slot = order_s[t, i]
            seen = mask_v[slot] > 0
            value = jnp.where(seen, rat_v[slot].astype(F32), 0.0)
            psm[i + 1] = psm[i] + jnp.where(seen, 1.0, 0.0)
            psr[i + 1] = psr[i] + value
            return carry

        lax.fori_loop(0, 32, body, 0)

    def dense(t):
        def body(r, carry):
            for c in range(8):
                begin, end = start_s[t, r * 8 + c], start_s[t, r * 8 + c + 1]
                weight = psm[end] - psm[begin]
                total = psr[end] - psr[begin]
                for b in range(2):
                    for f in range(2):
                        rows = slice(b * 64 + f * 32, b * 64 + f * 32 + 32)
                        at = pl.ds(pl.multiple_of(f * 512 + r * 64 + b * 32, 32), 32)
                        dm[at, c * 128:(c + 1) * 128] = weight[rows, :]
                        dr[at, c * 128:(c + 1) * 128] = total[rows, :]
            return carry

        lax.fori_loop(0, 8, body, 0)

    def remote(src, dst, send, recv, device):
        return pltpu.make_async_remote_copy(
            src_ref=src, dst_ref=dst, send_sem=send, recv_sem=recv, device_id=device, device_id_type=MESH)

    def rs_copy(f, src, dst, j):
        return (
            remote(rs_src.at[f, src], rs_dst.at[f, dst], rs_ss.at[f], rs_rs.at[f], (s, j)),
            remote(rs_src_sc.at[f, src], rs_dst_sc.at[f, dst], rs_ss2.at[f], rs_rs2.at[f], (s, j)),
        )

    def ag_copy(f, src, dst, j):
        return (
            remote(ag_src.at[f, src], ag_dst.at[f, dst], ag_ss.at[f], ag_rs.at[f], (s, j)),
            remote(ag_src_sc.at[f, src], ag_dst_sc.at[f, dst], ag_ss2.at[f], ag_rs2.at[f], (s, j)),
        )

    def all_of(make, f):
        most = pl.ds(0, n_dev - 1)
        return make(f, most, most, peer(1))

    def ag_send(f):
        rows = slice(f * 32, f * 32 + 32)
        code, scale = quantize(own[rows, :])
        ag_src[f, 0] = code
        ag_src_sc[f, 0] = scale
        for k in far_first:
            for copy in ag_copy(f, 0, d, peer(k)):
                copy.start()
        ag_dst[f, d] = code
        ag_dst_sc[f, d] = scale

    def ag_drain(f):
        for copy in all_of(ag_copy, f):
            copy.wait_send()

    def ag_take(f):
        for copy in all_of(ag_copy, f):
            copy.wait_recv()
        for j in range(n_dev):
            hi, low = split(decode(ag_dst[f, j], ag_dst_sc[f, j]))
            rows = slice(f * 512 + j * 32, f * 512 + j * 32 + 32)
            u3[rows, 0:128] = hi
            u3[rows, 128:256] = low
            u3[rows, 256:384] = hi

    def phase1(f):
        rows = slice(f * 512, f * 512 + 512)
        for c in range(4):
            cols = slice(c * 256, (c + 1) * 256)
            err = dm[rows, cols] * mm(u3[rows, :], h3[:, cols], NN) - dr[rows, cols]
            hi, low = split(err)
            e_hi[rows, cols] = hi
            e_lo[rows, cols] = low
        both = mm(e_hi[rows, :], hcat[...], NN)
        grad = both[:, 0:128] + both[:, 128:256] + mm(e_lo[rows, :], hcat[:, 0:128], NN)
        g_tile[...] = grad
        for j in range(n_dev):
            code, scale = quantize(grad[j * 32:j * 32 + 32, :])
            rs_src[f, j] = code
            rs_src_sc[f, j] = scale
        for k in far_first:
            for copy in rs_copy(f, peer(k), d, peer(k)):
                copy.start()
        g_own[f] = g_tile[pl.ds(pl.multiple_of(d * 32, 32), 32), :]

    def rs_sum(f):
        for copy in all_of(rs_copy, f):
            copy.wait_recv()
        total = g_own[f]
        for j in range(n_dev):
            total = total + decode(rs_dst[f, j], rs_dst_sc[f, j])
        rows = slice(f * 32, f * 32 + 32)
        own[rows, :] = SHRINK * own[rows, :] - LEARN_RATE * total

    def rs_drain(f):
        for copy in all_of(rs_copy, f):
            copy.wait_send()

    def h_copy(t, part):
        return (
            remote(h_src.at[part], h_dst.at[t, part], h_ss.at[t], h_rs.at[t], (ahead, d)),
            remote(h_src_sc.at[part], h_dst_sc.at[t, part], h_ss2.at[t], h_rs2.at[t], (ahead, d)),
        )

    def phase2(t):
        def body(c, carry):
            cols = pl.ds(pl.multiple_of(c * 128, 128), 128)
            both = mm(e_hi[:, cols], u3[:, 0:256], TN)
            grad = both[:, 0:128] + both[:, 128:256] + mm(e_lo[:, cols], u3[:, 0:128], TN)
            code, scale = quantize(SHRINK * hcur[cols, :] - LEARN_RATE * grad)
            h_src[c] = code
            h_src_sc[c] = scale
            for copy in h_copy(t, c):
                copy.start()
            return carry

        lax.fori_loop(0, 8, body, 0)

    load(0)
    own[...] = own_ref[...]
    pl.semaphore_wait(barrier, n_dev + 1)
    for f in range(2):
        ag_send(f)
    psm[0] = jnp.zeros_like(psm[0])
    psr[0] = jnp.zeros_like(psr[0])
    for f in range(2):
        rs_dst[f, d] = jnp.zeros((32, 128), I16)
        rs_dst_sc[f, d] = jnp.zeros((1, 128), F32)
    set_h(lambda c, rows: h0_ref[rows, :], True)
    prefix(0)
    load(1)
    dense(0)
    ag_take(0)

    def stratum(t, carry):
        more = t + 1 < STRATA
        phase1(0)
        ag_take(1)
        phase1(1)
        phase2(t)
        rs_sum(0)
        ag_drain(0)

        @pl.when(more)
        def _():
            ag_send(0)
            prefix(t + 1)

        rs_sum(1)
        ag_drain(1)

        @pl.when(more)
        def _():
            ag_send(1)
            dense(t + 1)

        @pl.when(t + 2 < STRATA)
        def _():
            load(t + 2)

        for f in range(2):
            rs_drain(f)
        for copy in h_copy(t, pl.ds(0, 8)):
            copy.wait()

        @pl.when(more)
        def _():
            set_h(lambda c, rows: decode(h_dst[t, c], h_dst_sc[t, c]), True)
            ag_take(0)

        return carry

    lax.fori_loop(0, STRATA, stratum, 0)
    uout_ref[...] = own[...]
    code_ref[...] = h_dst[STRATA - 1]
    scale_ref[...] = h_dst_sc[STRATA - 1]


def finish(own_ref, code_ref, scale_ref, uout_ref, hout_ref):
    uout_ref[...] = own_ref[...]
    for c in range(8):
        hout_ref[c * 128:(c + 1) * 128, :] = decode(code_ref[c], scale_ref[c])


def tile_lists(tile_rows, tile_cols, tile_count):
    slots = tile_rows.shape[1]
    index = jnp.arange(slots, dtype=jnp.int32)
    key = jnp.where(index[None, :] < tile_count, tile_rows * 8 + tile_cols, 64)
    unique = key * slots + index[None, :]
    rank = jnp.sum((unique[:, None, :] < unique[:, :, None]).astype(jnp.int32), axis=2)
    order = jnp.sum(jnp.where(rank[:, None, :] == index[None, :, None], index[None, None, :], 0), axis=2)
    cells = jnp.arange(72, dtype=jnp.int32)
    start = jnp.sum((key[:, None, :] < cells[None, :, None]).astype(jnp.int32), axis=2)
    return order, start


def shards(n_stripe, n_dev, row_factors, col_factors, ratings, rating_mask, tile_rows, tile_cols, tile_count):
    order, start = tile_lists(tile_rows, tile_cols, tile_count)
    vmem, smem, anywhere = (pl.BlockSpec(memory_space=m) for m in (pltpu.VMEM, pltpu.SMEM, pl.ANY))
    dma = lambda n: pltpu.SemaphoreType.DMA((n,))
    own, code, scale = pl.pallas_call(
        functools.partial(kernel, n_stripe, n_dev),
        out_shape=(
            jax.ShapeDtypeStruct(row_factors.shape, F32),
            jax.ShapeDtypeStruct((8, 128, 128), I16),
            jax.ShapeDtypeStruct((8, 1, 128), F32),
        ),
        in_specs=[smem, smem, vmem, vmem, anywhere, anywhere],
        out_specs=(vmem, vmem, vmem),
        scratch_shapes=[
            pltpu.VMEM((32, 128, 128), BF16),
            pltpu.VMEM((32, 128, 128), jnp.int32),
            *[pltpu.VMEM((33, 128, 128), F32)] * 2,
            *[pltpu.VMEM((1024, 1024), F32)] * 2,
            pltpu.VMEM((1024, 384), BF16),
            pltpu.VMEM((384, 1024), BF16),
            pltpu.VMEM((1024, 256), BF16),
            *[pltpu.VMEM((1024, 1024), BF16)] * 2,
            pltpu.VMEM((1024, 128), F32),
            pltpu.VMEM((64, 128), F32),
            pltpu.VMEM((512, 128), F32),
            pltpu.VMEM((2, 32, 128), F32),
            *[pltpu.VMEM((2, 16, 32, 128), I16), pltpu.VMEM((2, 16, 1, 128), F32)] * 2,
            pltpu.VMEM((2, 15, 32, 128), I16),
            pltpu.VMEM((2, 15, 1, 128), F32),
            pltpu.VMEM((2, 16, 32, 128), I16),
            pltpu.VMEM((2, 16, 1, 128), F32),
            pltpu.VMEM((8, 128, 128), I16),
            pltpu.VMEM((8, 1, 128), F32),
            pltpu.VMEM((3, 8, 128, 128), I16),
            pltpu.VMEM((3, 8, 1, 128), F32),
            *[dma(2)] * 9,
            *[dma(3)] * 4,
        ],
        compiler_params=pltpu.CompilerParams(
            collective_id=0, has_side_effects=True, vmem_limit_bytes=56 * 1024 * 1024
        ),
    )(order, start, row_factors, col_factors, ratings, rating_mask)
    return pl.pallas_call(
        finish,
        out_shape=(
            jax.ShapeDtypeStruct(row_factors.shape, F32),
            jax.ShapeDtypeStruct(col_factors.shape, F32),
        ),
        in_specs=[vmem] * 3,
        out_specs=(vmem, vmem),
        compiler_params=pltpu.CompilerParams(vmem_limit_bytes=16 * 1024 * 1024),
    )(own, code, scale)


def solution(mesh):
    in_specs = (
        P(("stripe", "dev"), None),
        P(("stripe", "dev"), None),
        P(None, ("stripe", "dev"), None, None),
        P(None, ("stripe", "dev"), None, None),
        P(None, ("stripe", "dev")),
        P(None, ("stripe", "dev")),
        P(None, ("stripe", "dev")),
    )
    out_specs = (P(("stripe", "dev"), None), P(("stripe", "dev"), None))
    body = functools.partial(shards, mesh.shape["stripe"], mesh.shape["dev"])
    return jax.shard_map(body, mesh=mesh, in_specs=in_specs, out_specs=out_specs, check_vma=False)
```

```python
import functools

import jax
import jax.numpy as jnp
from jax import lax
from jax.experimental import pallas as pl
from jax.experimental.pallas import tpu as pltpu
from jax.sharding import PartitionSpec as P

MESH = pl.DeviceIdType.MESH
STRATA = 3
LEARN_RATE = 0.02
RIDGE_WEIGHT = 2.5
SHRINK = 1.0 - LEARN_RATE * RIDGE_WEIGHT
F32, BF16, I16 = jnp.float32, jnp.bfloat16, jnp.int16
TOP = 32767.0
NT = (((1,), (1,)), ((), ()))
NN = (((1,), (0,)), ((), ()))
TN = (((0,), (0,)), ((), ()))


def mm(a, b, dims):
    return lax.dot_general(a, b, dims, preferred_element_type=F32)


def split(x):
    hi = x.astype(BF16)
    return hi, (x - hi.astype(F32)).astype(BF16)


def quantize(x):
    peak = jnp.maximum(jnp.max(jnp.abs(x), axis=0, keepdims=True), 1e-30)
    code = jnp.round(x * (TOP / peak)).astype(jnp.int32).astype(I16)
    return code, peak * (1.0 / TOP)


def decode(code, scale):
    return code.astype(jnp.int32).astype(F32) * scale


def tile_lists(tile_rows, tile_cols, tile_count, out):
    slots = tile_rows.shape[1]
    index = lax.broadcasted_iota(jnp.int32, (STRATA, slots), 1)
    key = tile_rows[...] * 8 + tile_cols[...]
    across = lax.broadcasted_iota(jnp.int32, (slots, slots), 1)
    down = lax.broadcasted_iota(jnp.int32, (slots, slots), 0)
    place = lax.broadcasted_iota(jnp.int32, (slots, 128), 1)
    slot = lax.broadcasted_iota(jnp.int32, (slots, 128), 0)
    for t in range(STRATA):
        line = jnp.where(index[0:1, :] < tile_count[t], key[t:t + 1, :], 64) * slots + index[0:1, :]
        line = jnp.broadcast_to(line, (slots, slots))
        column = jnp.sum(jnp.where(across == down, line, 0), axis=1, keepdims=True)
        rank = jnp.sum(jnp.where(line < column, 1, 0), axis=1, keepdims=True)
        out[t:t + 1, :] = jnp.sum(jnp.where(rank == place, slot, 0), axis=0, keepdims=True)
        out[4 + t:5 + t, :] = jnp.sum(jnp.where(column < place * slots, 1, 0), axis=0, keepdims=True)


def kernel(
    n_stripe, n_dev, tr_ref, tc_ref, count_ref, own_ref, h0_ref, rat_ref, mask_ref, uout_ref, code_ref, scale_ref,
    list_v, list_s, rat_v, mask_v, psm, psr, dm, dr, u3, h3, hcat, e_hi, e_lo, hcur, own, g_tile, g_own,
    rs_src, rs_src_sc, rs_dst, rs_dst_sc, ag_src, ag_src_sc, ag_dst, ag_dst_sc, h_src, h_src_sc, h_dst, h_dst_sc,
    in_sem, rs_ss, rs_rs, rs_ss2, rs_rs2, ag_ss, ag_rs, ag_ss2, ag_rs2, h_ss, h_rs, h_ss2, h_rs2,
):
    s, d = lax.axis_index("stripe"), lax.axis_index("dev")
    ahead = lax.rem(s + 1, n_stripe)
    behind = lax.rem(s + n_stripe - 1, n_stripe)
    far_first = (8, 9, 7, 6, 10, 5, 11, 4, 12, 3, 13, 2, 14, 1, 15)

    def peer(k):
        return lax.rem(d + k, n_dev)

    barrier = pltpu.get_barrier_semaphore()
    for k in range(1, n_dev):
        pl.semaphore_signal(barrier, inc=1, device_id=(s, peer(k)), device_id_type=MESH)
    for other in (ahead, behind):
        pl.semaphore_signal(barrier, inc=1, device_id=(other, d), device_id_type=MESH)

    def loads(t):
        return (
            pltpu.make_async_copy(rat_ref.at[t], rat_v, in_sem.at[0]),
            pltpu.make_async_copy(mask_ref.at[t], mask_v, in_sem.at[1]),
        )

    def load(t):
        for copy in loads(t):
            copy.start()

    def set_h(value, save):
        def body(c, carry):
            rows = pl.ds(pl.multiple_of(c * 128, 128), 128)
            x = value(c, rows)
            if save:
                hcur[rows, :] = x
            hi, low = split(x)
            hcat[rows, 0:128] = hi
            hcat[rows, 128:256] = low
            hi, low = split(x.T)
            h3[0:128, rows] = hi
            h3[128:256, rows] = hi
            h3[256:384, rows] = low
            return carry

        lax.fori_loop(0, 8, body, 0)

    def prefix(t):
        for copy in loads(t):
            copy.wait()

        def body(i, carry):
            slot = list_s[t, i]
            seen = mask_v[slot] > 0
            value = jnp.where(seen, rat_v[slot].astype(F32), 0.0)
            psm[i + 1] = psm[i] + jnp.where(seen, 1.0, 0.0)
            psr[i + 1] = psr[i] + value
            return carry

        lax.fori_loop(0, 32, body, 0)

    def dense(t):
        def body(r, carry):
            for c in range(8):
                begin, end = list_s[4 + t, r * 8 + c], list_s[4 + t, r * 8 + c + 1]
                weight = psm[end] - psm[begin]
                total = psr[end] - psr[begin]
                for b in range(2):
                    for f in range(2):
                        rows = slice(b * 64 + f * 32, b * 64 + f * 32 + 32)
                        at = pl.ds(pl.multiple_of(f * 512 + r * 64 + b * 32, 32), 32)
                        dm[at, c * 128:(c + 1) * 128] = weight[rows, :]
                        dr[at, c * 128:(c + 1) * 128] = total[rows, :]
            return carry

        lax.fori_loop(0, 8, body, 0)

    def remote(src, dst, send, recv, device):
        return pltpu.make_async_remote_copy(
            src_ref=src, dst_ref=dst, send_sem=send, recv_sem=recv, device_id=device, device_id_type=MESH)

    def rs_copy(f, src, dst, j):
        return (
            remote(rs_src.at[f, src], rs_dst.at[f, dst], rs_ss.at[f], rs_rs.at[f], (s, j)),
            remote(rs_src_sc.at[f, src], rs_dst_sc.at[f, dst], rs_ss2.at[f], rs_rs2.at[f], (s, j)),
        )

    def ag_copy(f, src, dst, j):
        return (
            remote(ag_src.at[f, src], ag_dst.at[f, dst], ag_ss.at[f], ag_rs.at[f], (s, j)),
            remote(ag_src_sc.at[f, src], ag_dst_sc.at[f, dst], ag_ss2.at[f], ag_rs2.at[f], (s, j)),
        )

    def all_of(make, f):
        most = pl.ds(0, n_dev - 1)
        return make(f, most, most, peer(1))

    def ag_send(f):
        rows = slice(f * 32, f * 32 + 32)
        code, scale = quantize(own[rows, :])
        ag_src[f, 0] = code
        ag_src_sc[f, 0] = scale
        for k in far_first:
            for copy in ag_copy(f, 0, d, peer(k)):
                copy.start()
        ag_dst[f, d] = code
        ag_dst_sc[f, d] = scale

    def ag_drain(f):
        for copy in all_of(ag_copy, f):
            copy.wait_send()

    def ag_take(f):
        for copy in all_of(ag_copy, f):
            copy.wait_recv()
        for j in range(n_dev):
            hi, low = split(decode(ag_dst[f, j], ag_dst_sc[f, j]))
            rows = slice(f * 512 + j * 32, f * 512 + j * 32 + 32)
            u3[rows, 0:128] = hi
            u3[rows, 128:256] = low
            u3[rows, 256:384] = hi

    def phase1(f):
        rows = slice(f * 512, f * 512 + 512)
        for c in range(4):
            cols = slice(c * 256, (c + 1) * 256)
            err = dm[rows, cols] * mm(u3[rows, :], h3[:, cols], NN) - dr[rows, cols]
            hi, low = split(err)
            e_hi[rows, cols] = hi
            e_lo[rows, cols] = low
        both = mm(e_hi[rows, :], hcat[...], NN)
        grad = both[:, 0:128] + both[:, 128:256] + mm(e_lo[rows, :], hcat[:, 0:128], NN)
        g_tile[...] = grad
        for j in range(n_dev):
            code, scale = quantize(grad[j * 32:j * 32 + 32, :])
            rs_src[f, j] = code
            rs_src_sc[f, j] = scale
        for k in far_first:
            for copy in rs_copy(f, peer(k), d, peer(k)):
                copy.start()
        g_own[f] = g_tile[pl.ds(pl.multiple_of(d * 32, 32), 32), :]

    def rs_sum(f):
        for copy in all_of(rs_copy, f):
            copy.wait_recv()
        total = g_own[f]
        for j in range(n_dev):
            total = total + decode(rs_dst[f, j], rs_dst_sc[f, j])
        rows = slice(f * 32, f * 32 + 32)
        own[rows, :] = SHRINK * own[rows, :] - LEARN_RATE * total

    def rs_drain(f):
        for copy in all_of(rs_copy, f):
            copy.wait_send()

    def h_copy(t, part):
        return (
            remote(h_src.at[part], h_dst.at[t, part], h_ss.at[t], h_rs.at[t], (ahead, d)),
            remote(h_src_sc.at[part], h_dst_sc.at[t, part], h_ss2.at[t], h_rs2.at[t], (ahead, d)),
        )

    def phase2(t):
        def body(c, carry):
            cols = pl.ds(pl.multiple_of(c * 128, 128), 128)
            both = mm(e_hi[:, cols], u3[:, 0:256], TN)
            grad = both[:, 0:128] + both[:, 128:256] + mm(e_lo[:, cols], u3[:, 0:128], TN)
            code, scale = quantize(SHRINK * hcur[cols, :] - LEARN_RATE * grad)
            h_src[c] = code
            h_src_sc[c] = scale
            for copy in h_copy(t, c):
                copy.start()
            return carry

        lax.fori_loop(0, 8, body, 0)

    load(0)
    own[...] = own_ref[...]
    pl.semaphore_wait(barrier, n_dev + 1)
    for f in range(2):
        ag_send(f)
    tile_lists(tr_ref, tc_ref, count_ref, list_v)
    to_scalars = pltpu.make_async_copy(list_v, list_s, in_sem.at[2])
    to_scalars.start()
    psm[0] = jnp.zeros_like(psm[0])
    psr[0] = jnp.zeros_like(psr[0])
    for f in range(2):
        rs_dst[f, d] = jnp.zeros((32, 128), I16)
        rs_dst_sc[f, d] = jnp.zeros((1, 128), F32)
    set_h(lambda c, rows: h0_ref[rows, :], True)
    to_scalars.wait()
    prefix(0)
    load(1)
    dense(0)
    ag_take(0)

    def stratum(t, carry):
        more = t + 1 < STRATA
        phase1(0)
        ag_take(1)
        phase1(1)
        phase2(t)
        rs_sum(0)
        ag_drain(0)

        @pl.when(more)
        def _():
            ag_send(0)
            prefix(t + 1)

        rs_sum(1)
        ag_drain(1)

        @pl.when(more)
        def _():
            ag_send(1)
            dense(t + 1)

        @pl.when(t + 2 < STRATA)
        def _():
            load(t + 2)

        for f in range(2):
            rs_drain(f)
        for copy in h_copy(t, pl.ds(0, 8)):
            copy.wait()

        @pl.when(more)
        def _():
            set_h(lambda c, rows: decode(h_dst[t, c], h_dst_sc[t, c]), True)
            ag_take(0)

        return carry

    lax.fori_loop(0, STRATA, stratum, 0)
    uout_ref[...] = own[...]
    code_ref[...] = h_dst[STRATA - 1]
    scale_ref[...] = h_dst_sc[STRATA - 1]


def finish(own_ref, code_ref, scale_ref, uout_ref, hout_ref, code, scale, sems):
    copies = (
        pltpu.make_async_copy(code_ref, code, sems.at[0]),
        pltpu.make_async_copy(scale_ref, scale, sems.at[1]),
        pltpu.make_async_copy(own_ref, uout_ref, sems.at[2]),
    )
    for copy in copies:
        copy.start()
    for copy in copies:
        copy.wait()
    for c in range(8):
        hout_ref[c * 128:(c + 1) * 128, :] = decode(code[c], scale[c])


def shards(n_stripe, n_dev, row_factors, col_factors, ratings, rating_mask, tile_rows, tile_cols, tile_count):
    vmem, smem, anywhere = (pl.BlockSpec(memory_space=m) for m in (pltpu.VMEM, pltpu.SMEM, pl.ANY))
    dma = lambda n: pltpu.SemaphoreType.DMA((n,))
    own, code, scale = pl.pallas_call(
        functools.partial(kernel, n_stripe, n_dev),
        out_shape=(
            jax.ShapeDtypeStruct(row_factors.shape, F32),
            jax.ShapeDtypeStruct((8, 128, 128), I16),
            jax.ShapeDtypeStruct((8, 1, 128), F32),
        ),
        in_specs=[vmem, vmem, smem, vmem, vmem, anywhere, anywhere],
        out_specs=(vmem, vmem, vmem),
        scratch_shapes=[
            pltpu.VMEM((8, 128), jnp.int32),
            pltpu.SMEM((8, 128), jnp.int32),
            pltpu.VMEM((32, 128, 128), BF16),
            pltpu.VMEM((32, 128, 128), jnp.int32),
            *[pltpu.VMEM((33, 128, 128), F32)] * 2,
            *[pltpu.VMEM((1024, 1024), F32)] * 2,
            pltpu.VMEM((1024, 384), BF16),
            pltpu.VMEM((384, 1024), BF16),
            pltpu.VMEM((1024, 256), BF16),
            *[pltpu.VMEM((1024, 1024), BF16)] * 2,
            pltpu.VMEM((1024, 128), F32),
            pltpu.VMEM((64, 128), F32),
            pltpu.VMEM((512, 128), F32),
            pltpu.VMEM((2, 32, 128), F32),
            *[pltpu.VMEM((2, 16, 32, 128), I16), pltpu.VMEM((2, 16, 1, 128), F32)] * 2,
            pltpu.VMEM((2, 15, 32, 128), I16),
            pltpu.VMEM((2, 15, 1, 128), F32),
            pltpu.VMEM((2, 16, 32, 128), I16),
            pltpu.VMEM((2, 16, 1, 128), F32),
            pltpu.VMEM((8, 128, 128), I16),
            pltpu.VMEM((8, 1, 128), F32),
            pltpu.VMEM((3, 8, 128, 128), I16),
            pltpu.VMEM((3, 8, 1, 128), F32),
            dma(3),
            *[dma(2)] * 8,
            *[dma(3)] * 4,
        ],
        compiler_params=pltpu.CompilerParams(
            collective_id=0, has_side_effects=True, vmem_limit_bytes=56 * 1024 * 1024
        ),
    )(tile_rows, tile_cols, tile_count.reshape(STRATA), row_factors, col_factors, ratings, rating_mask)
    return pl.pallas_call(
        finish,
        out_shape=(
            jax.ShapeDtypeStruct(row_factors.shape, F32),
            jax.ShapeDtypeStruct(col_factors.shape, F32),
        ),
        in_specs=[anywhere] * 3,
        out_specs=(vmem, vmem),
        scratch_shapes=[pltpu.VMEM((8, 128, 128), I16), pltpu.VMEM((8, 1, 128), F32), dma(3)],
        compiler_params=pltpu.CompilerParams(vmem_limit_bytes=63400000),
    )(own, code, scale)


def solution(mesh):
    in_specs = (
        P(("stripe", "dev"), None),
        P(("stripe", "dev"), None),
        P(None, ("stripe", "dev"), None, None),
        P(None, ("stripe", "dev"), None, None),
        P(None, ("stripe", "dev")),
        P(None, ("stripe", "dev")),
        P(None, ("stripe", "dev")),
    )
    out_specs = (P(("stripe", "dev"), None), P(("stripe", "dev"), None))
    body = functools.partial(shards, mesh.shape["stripe"], mesh.shape["dev"])
    return jax.shard_map(body, mesh=mesh, in_specs=in_specs, out_specs=out_specs, check_vma=False)
```

```python
import functools

import jax
import jax.numpy as jnp
from jax import lax
from jax.experimental import pallas as pl
from jax.experimental.pallas import tpu as pltpu
from jax.sharding import PartitionSpec as P

MESH = pl.DeviceIdType.MESH
STRATA = 3
PARTS = 4
LEARN_RATE = 0.02
RIDGE_WEIGHT = 2.5
SHRINK = 1.0 - LEARN_RATE * RIDGE_WEIGHT
F32, BF16, I16 = jnp.float32, jnp.bfloat16, jnp.int16
TOP = 32767.0
NT = (((1,), (1,)), ((), ()))
NN = (((1,), (0,)), ((), ()))
TN = (((0,), (0,)), ((), ()))


def mm(a, b, dims):
    return lax.dot_general(a, b, dims, preferred_element_type=F32)


def split(x):
    hi = x.astype(BF16)
    return hi, (x - hi.astype(F32)).astype(BF16)


def quantize(x):
    peak = jnp.maximum(jnp.max(jnp.abs(x), axis=0, keepdims=True), 1e-30)
    code = jnp.round(x * (TOP / peak)).astype(jnp.int32).astype(I16)
    return code, peak * (1.0 / TOP)


def decode(code, scale):
    return code.astype(jnp.int32).astype(F32) * scale


def tile_lists(tile_rows, tile_cols, tile_count, out):
    slots = tile_rows.shape[1]
    index = lax.broadcasted_iota(jnp.int32, (STRATA, slots), 1)
    key = tile_rows[...] * 8 + tile_cols[...]
    across = lax.broadcasted_iota(jnp.int32, (slots, slots), 1)
    down = lax.broadcasted_iota(jnp.int32, (slots, slots), 0)
    place = lax.broadcasted_iota(jnp.int32, (slots, 128), 1)
    slot = lax.broadcasted_iota(jnp.int32, (slots, 128), 0)
    for t in range(STRATA):
        line = jnp.where(index[0:1, :] < tile_count[t], key[t:t + 1, :], 64) * slots + index[0:1, :]
        line = jnp.broadcast_to(line, (slots, slots))
        column = jnp.sum(jnp.where(across == down, line, 0), axis=1, keepdims=True)
        rank = jnp.sum(jnp.where(line < column, 1, 0), axis=1, keepdims=True)
        out[t:t + 1, :] = jnp.sum(jnp.where(rank == place, slot, 0), axis=0, keepdims=True)
        out[4 + t:5 + t, :] = jnp.sum(jnp.where(column < place * slots, 1, 0), axis=0, keepdims=True)


def kernel(
    n_stripe, n_dev, tr_ref, tc_ref, count_ref, own_ref, h0_ref, rat_ref, mask_ref, uout_ref, code_ref, scale_ref,
    list_v, list_s, rat_v, mask_v, psm, psr, dm, dr, u3, h3, hcat, e_hi, e_lo, hcur, own, g_tile, g_own,
    rs_src, rs_src_sc, rs_dst, rs_dst_sc, ag_src, ag_src_sc, ag_dst, ag_dst_sc, h_src, h_src_sc, h_dst, h_dst_sc,
    in_sem, rs_ss, rs_rs, rs_ss2, rs_rs2, ag_ss, ag_rs, ag_ss2, ag_rs2, h_ss, h_rs, h_ss2, h_rs2,
):
    s, d = lax.axis_index("stripe"), lax.axis_index("dev")
    ahead = lax.rem(s + 1, n_stripe)
    behind = lax.rem(s + n_stripe - 1, n_stripe)
    far_first = (8, 9, 7, 6, 10, 5, 11, 4, 12, 3, 13, 2, 14, 1, 15)

    def peer(k):
        return lax.rem(d + k, n_dev)

    barrier = pltpu.get_barrier_semaphore()
    for k in range(1, n_dev):
        pl.semaphore_signal(barrier, inc=1, device_id=(s, peer(k)), device_id_type=MESH)
    for other in (ahead, behind):
        pl.semaphore_signal(barrier, inc=1, device_id=(other, d), device_id_type=MESH)

    def loads(t):
        return (
            pltpu.make_async_copy(rat_ref.at[t], rat_v, in_sem.at[0]),
            pltpu.make_async_copy(mask_ref.at[t], mask_v, in_sem.at[1]),
        )

    def load(t):
        for copy in loads(t):
            copy.start()

    def set_h(value, save):
        def body(c, carry):
            rows = pl.ds(pl.multiple_of(c * 128, 128), 128)
            x = value(c, rows)
            if save:
                hcur[rows, :] = x
            hi, low = split(x)
            hcat[rows, 0:128] = hi
            hcat[rows, 128:256] = low
            hi, low = split(x.T)
            h3[0:128, rows] = hi
            h3[128:256, rows] = hi
            h3[256:384, rows] = low
            return carry

        lax.fori_loop(0, 8, body, 0)

    def prefix(t):
        for copy in loads(t):
            copy.wait()

        def body(i, carry):
            slot = list_s[t, i]
            seen = mask_v[slot] > 0
            value = jnp.where(seen, rat_v[slot].astype(F32), 0.0)
            psm[i + 1] = psm[i] + jnp.where(seen, 1.0, 0.0)
            psr[i + 1] = psr[i] + value
            return carry

        lax.fori_loop(0, 32, body, 0)

    def dense(t):
        def body(r, carry):
            for c in range(8):
                begin, end = list_s[4 + t, r * 8 + c], list_s[4 + t, r * 8 + c + 1]
                weight = psm[end] - psm[begin]
                total = psr[end] - psr[begin]
                for b in range(2):
                    for f in range(PARTS):
                        rows = slice(b * 64 + f * 16, b * 64 + f * 16 + 16)
                        at = pl.ds(pl.multiple_of(f * 256 + r * 32 + b * 16, 16), 16)
                        dm[at, c * 128:(c + 1) * 128] = weight[rows, :]
                        dr[at, c * 128:(c + 1) * 128] = total[rows, :]
            return carry

        lax.fori_loop(0, 8, body, 0)

    def remote(src, dst, send, recv, device):
        return pltpu.make_async_remote_copy(
            src_ref=src, dst_ref=dst, send_sem=send, recv_sem=recv, device_id=device, device_id_type=MESH)

    def rs_copy(f, src, dst, j):
        return (
            remote(rs_src.at[f, src], rs_dst.at[f, dst], rs_ss.at[f], rs_rs.at[f], (s, j)),
            remote(rs_src_sc.at[f, src], rs_dst_sc.at[f, dst], rs_ss2.at[f], rs_rs2.at[f], (s, j)),
        )

    def ag_copy(f, src, dst, j):
        return (
            remote(ag_src.at[f, src], ag_dst.at[f, dst], ag_ss.at[f], ag_rs.at[f], (s, j)),
            remote(ag_src_sc.at[f, src], ag_dst_sc.at[f, dst], ag_ss2.at[f], ag_rs2.at[f], (s, j)),
        )

    def all_of(make, f):
        most = pl.ds(0, n_dev - 1)
        return make(f, most, most, peer(1))

    def ag_send(f):
        rows = slice(f * 16, f * 16 + 16)
        code, scale = quantize(own[rows, :])
        ag_src[f, 0] = code
        ag_src_sc[f, 0] = scale
        for k in far_first:
            for copy in ag_copy(f, 0, d, peer(k)):
                copy.start()
        ag_dst[f, d] = code
        ag_dst_sc[f, d] = scale

    def ag_drain(f):
        for copy in all_of(ag_copy, f):
            copy.wait_send()

    def ag_take(f):
        for copy in all_of(ag_copy, f):
            copy.wait_recv()
        for j in range(n_dev):
            hi, low = split(decode(ag_dst[f, j], ag_dst_sc[f, j]))
            rows = slice(f * 256 + j * 16, f * 256 + j * 16 + 16)
            u3[rows, 0:128] = hi
            u3[rows, 128:256] = low
            u3[rows, 256:384] = hi

    def phase1(f):
        rows = slice(f * 256, f * 256 + 256)
        for c in range(4):
            cols = slice(c * 256, (c + 1) * 256)
            err = dm[rows, cols] * mm(u3[rows, :], h3[:, cols], NN) - dr[rows, cols]
            hi, low = split(err)
            e_hi[rows, cols] = hi
            e_lo[rows, cols] = low
        both = mm(e_hi[rows, :], hcat[...], NN)
        grad = both[:, 0:128] + both[:, 128:256] + mm(e_lo[rows, :], hcat[:, 0:128], NN)
        g_tile[...] = grad
        for j in range(n_dev):
            code, scale = quantize(grad[j * 16:j * 16 + 16, :])
            rs_src[f, j] = code
            rs_src_sc[f, j] = scale
        for k in far_first:
            for copy in rs_copy(f, peer(k), d, peer(k)):
                copy.start()
        g_own[f] = g_tile[pl.ds(pl.multiple_of(d * 16, 16), 16), :]

    def rs_sum(f):
        for copy in all_of(rs_copy, f):
            copy.wait_recv()
        total = g_own[f]
        for j in range(n_dev):
            total = total + decode(rs_dst[f, j], rs_dst_sc[f, j])
        rows = slice(f * 16, f * 16 + 16)
        own[rows, :] = SHRINK * own[rows, :] - LEARN_RATE * total

    def rs_drain(f):
        for copy in all_of(rs_copy, f):
            copy.wait_send()

    def h_copy(t, part):
        sem = 8 * t + part
        return (
            remote(h_src.at[part], h_dst.at[t, part], h_ss.at[sem], h_rs.at[sem], (ahead, d)),
            remote(h_src_sc.at[part], h_dst_sc.at[t, part], h_ss2.at[sem], h_rs2.at[sem], (ahead, d)),
        )

    def h_landed(t, part):
        for copy in h_copy(t, part):
            copy.wait_recv()
        return decode(h_dst[t, part], h_dst_sc[t, part])

    def phase2(t):
        def body(c, carry):
            cols = pl.ds(pl.multiple_of(c * 128, 128), 128)
            both = mm(e_hi[:, cols], u3[:, 0:256], TN)
            grad = both[:, 0:128] + both[:, 128:256] + mm(e_lo[:, cols], u3[:, 0:128], TN)
            code, scale = quantize(SHRINK * hcur[cols, :] - LEARN_RATE * grad)
            h_src[c] = code
            h_src_sc[c] = scale
            for copy in h_copy(t, c):
                copy.start()
            return carry

        lax.fori_loop(0, 8, body, 0)

    load(0)
    own[...] = own_ref[...]
    pl.semaphore_wait(barrier, n_dev + 1)
    for f in range(PARTS):
        ag_send(f)
    tile_lists(tr_ref, tc_ref, count_ref, list_v)
    to_scalars = pltpu.make_async_copy(list_v, list_s, in_sem.at[2])
    to_scalars.start()
    psm[0] = jnp.zeros_like(psm[0])
    psr[0] = jnp.zeros_like(psr[0])
    for f in range(PARTS):
        rs_dst[f, d] = jnp.zeros((16, 128), I16)
        rs_dst_sc[f, d] = jnp.zeros((1, 128), F32)
    set_h(lambda c, rows: h0_ref[rows, :], True)
    to_scalars.wait()
    prefix(0)
    load(1)
    dense(0)
    ag_take(0)

    def stratum(t, carry):
        more = t + 1 < STRATA
        phase1(0)
        for f in range(1, PARTS):
            ag_take(f)
            phase1(f)
        phase2(t)
        for f in range(PARTS):
            rs_sum(f)
            ag_drain(f)

            @pl.when(more)
            def _():
                ag_send(f)


        @pl.when(more)
        def _():
            prefix(t + 1)
            dense(t + 1)

        @pl.when(t + 2 < STRATA)
        def _():
            load(t + 2)

        for f in range(PARTS):
            rs_drain(f)
        @pl.when(more)
        def _():
            set_h(lambda c, rows: h_landed(t, c), True)
            ag_take(0)

        def sent(c, carry):
            for copy in h_copy(t, c):
                copy.wait_send()
            return carry

        lax.fori_loop(0, 8, sent, 0)

        return carry

    lax.fori_loop(0, STRATA, stratum, 0)
    uout_ref[...] = own[...]
    for c in range(8):
        for copy in h_copy(STRATA - 1, c):
            copy.wait_recv()
        code_ref[c] = h_dst[STRATA - 1, c]
        scale_ref[c] = h_dst_sc[STRATA - 1, c]


def finish(own_ref, code_ref, scale_ref, uout_ref, hout_ref, code, scale, sems):
    copies = (
        pltpu.make_async_copy(code_ref, code, sems.at[0]),
        pltpu.make_async_copy(scale_ref, scale, sems.at[1]),
        pltpu.make_async_copy(own_ref, uout_ref, sems.at[2]),
    )
    for copy in copies:
        copy.start()
    for copy in copies:
        copy.wait()
    for c in range(8):
        hout_ref[c * 128:(c + 1) * 128, :] = decode(code[c], scale[c])


def shards(n_stripe, n_dev, row_factors, col_factors, ratings, rating_mask, tile_rows, tile_cols, tile_count):
    vmem, smem, anywhere = (pl.BlockSpec(memory_space=m) for m in (pltpu.VMEM, pltpu.SMEM, pl.ANY))
    dma = lambda n: pltpu.SemaphoreType.DMA((n,))
    own, code, scale = pl.pallas_call(
        functools.partial(kernel, n_stripe, n_dev),
        out_shape=(
            jax.ShapeDtypeStruct(row_factors.shape, F32),
            jax.ShapeDtypeStruct((8, 128, 128), I16),
            jax.ShapeDtypeStruct((8, 1, 128), F32),
        ),
        in_specs=[vmem, vmem, smem, vmem, vmem, anywhere, anywhere],
        out_specs=(vmem, vmem, vmem),
        scratch_shapes=[
            pltpu.VMEM((8, 128), jnp.int32),
            pltpu.SMEM((8, 128), jnp.int32),
            pltpu.VMEM((32, 128, 128), BF16),
            pltpu.VMEM((32, 128, 128), jnp.int32),
            *[pltpu.VMEM((33, 128, 128), F32)] * 2,
            *[pltpu.VMEM((1024, 1024), F32)] * 2,
            pltpu.VMEM((1024, 384), BF16),
            pltpu.VMEM((384, 1024), BF16),
            pltpu.VMEM((1024, 256), BF16),
            *[pltpu.VMEM((1024, 1024), BF16)] * 2,
            pltpu.VMEM((1024, 128), F32),
            pltpu.VMEM((64, 128), F32),
            pltpu.VMEM((256, 128), F32),
            pltpu.VMEM((PARTS, 16, 128), F32),
            *[pltpu.VMEM((PARTS, 16, 16, 128), I16), pltpu.VMEM((PARTS, 16, 1, 128), F32)] * 2,
            pltpu.VMEM((PARTS, 15, 16, 128), I16),
            pltpu.VMEM((PARTS, 15, 1, 128), F32),
            pltpu.VMEM((PARTS, 16, 16, 128), I16),
            pltpu.VMEM((PARTS, 16, 1, 128), F32),
            pltpu.VMEM((8, 128, 128), I16),
            pltpu.VMEM((8, 1, 128), F32),
            pltpu.VMEM((3, 8, 128, 128), I16),
            pltpu.VMEM((3, 8, 1, 128), F32),
            dma(3),
            *[dma(PARTS)] * 8,
            *[dma(24)] * 4,
        ],
        compiler_params=pltpu.CompilerParams(
            collective_id=0, has_side_effects=True, vmem_limit_bytes=56 * 1024 * 1024
        ),
    )(tile_rows, tile_cols, tile_count.reshape(STRATA), row_factors, col_factors, ratings, rating_mask)
    return pl.pallas_call(
        finish,
        out_shape=(
            jax.ShapeDtypeStruct(row_factors.shape, F32),
            jax.ShapeDtypeStruct(col_factors.shape, F32),
        ),
        in_specs=[anywhere] * 3,
        out_specs=(vmem, vmem),
        scratch_shapes=[pltpu.VMEM((8, 128, 128), I16), pltpu.VMEM((8, 1, 128), F32), dma(3)],
        compiler_params=pltpu.CompilerParams(vmem_limit_bytes=63400000),
    )(own, code, scale)


def solution(mesh):
    in_specs = (
        P(("stripe", "dev"), None),
        P(("stripe", "dev"), None),
        P(None, ("stripe", "dev"), None, None),
        P(None, ("stripe", "dev"), None, None),
        P(None, ("stripe", "dev")),
        P(None, ("stripe", "dev")),
        P(None, ("stripe", "dev")),
    )
    out_specs = (P(("stripe", "dev"), None), P(("stripe", "dev"), None))
    body = functools.partial(shards, mesh.shape["stripe"], mesh.shape["dev"])
    return jax.shard_map(body, mesh=mesh, in_specs=in_specs, out_specs=out_specs, check_vma=False)
```
